32 devices in a mesh: seq: 4 (over y, x), mem: 8 (over z, core).
Axes of the slice: x: 2, y: 2, z: 4, core: 2. Of those that a mesh axis runs over, the one named last changes fastest.
Arguments:
- queries: bfloat16 [512, 8192], P(('seq', 'mem')), may hold values from -90 to 90
- probes: int32 [512, 64, 8], P('seq'), may hold values from 0 to 15, as said below
- keys: bfloat16 [4, 4096, 8192], P('seq', 'mem'), may hold values from -5 to 5
- values: bfloat16 [4, 4096, 8192], P('seq', 'mem'), may hold values from -6 to 6
- w_out: bfloat16 [8192, 8192], P('mem', 'seq'), may hold values from -0.75 to 0.75
Outputs:
- output: bfloat16 [512, 8192], P(('seq', 'mem'))
The draws below stay inside these ranges and needn't reach their ends.
Inputs may be any that keep to these rules, and one draw needn't show every extreme that they name: `probes`: for each row and head the 8 ids are distinct blocks of the row's group memory.
All inputs are finite; a program needn't handle non-finite values.
Results may differ from the reference program's by a relative error of at most 0.023.
Values may be sent and summed in bfloat16 or wider, within the bound.
A program may use at most 256 MiB of HBM per device.

```python
import jax
import jax.numpy as jnp
from jax import lax

D = 8192
H = 64
DH = 128
BLOCK = 256
TOPB = 8
Q_DEV = 16
BLK_DEV = 2
MEMORY = 4096
N_SEQ = 4
N_MEM = 8


def probe_table(key):
    row_total = Q_DEV * N_MEM * N_SEQ
    block_count = BLK_DEV * N_MEM
    popular = jax.random.randint(jax.random.fold_in(key, 11), (block_count,), 0, 4) * 400
    noise = jax.random.randint(jax.random.fold_in(key, 12), (row_total, H, block_count), 0, 1024)
    scored = (noise + popular[None, None, :]) * block_count + jnp.arange(block_count, dtype=jnp.int32)
    return lax.top_k(scored, TOPB)[1].astype(jnp.int32)


def key_table(key):
    memory_keys = BLK_DEV * BLOCK * N_MEM
    normal_keys = jnp.clip(jax.random.normal(jax.random.fold_in(key, 21), (N_SEQ, memory_keys, D), jnp.float32), -4.0, 4.0)
    return normal_keys


def draw_probes(key, part):
    return probe_table(key)


def draw_keys(key, part):
    return key_table(key).astype(jnp.bfloat16)


def draw_queries(key, part):
    row_total = Q_DEV * N_MEM * N_SEQ
    drawn_rows = 1.5 * jnp.clip(jax.random.normal(jax.random.fold_in(key, 32), (row_total, D), jnp.float32), -4.0, 4.0)
    return drawn_rows.astype(jnp.bfloat16)


def shard_levels(rng, extent, shards, least, high):
    def one(dim, blocks):
        heights = jax.random.uniform(jax.random.fold_in(jax.random.fold_in(rng, 6), dim), (blocks,), jnp.float32, least / len(shards), high / len(shards))
        return jnp.repeat(jnp.exp(heights), extent[dim] // blocks).reshape((-1,) + (1,) * (len(extent) - dim - 1))

    level = one(*shards[0])
    for cut in shards[1:]:
        level = level * one(*cut)
    return level


def gaussian(rng, shape, deviation, reach, shards=(), kind=jnp.bfloat16):
    factor_of = shard_levels(rng, shape, shards, -0.22, 0.18) if shards else 1.0
    drawn = jax.random.normal(rng, shape, jnp.float32) * deviation * factor_of
    return jnp.minimum(jnp.maximum(drawn, -reach), reach).astype(kind)


def setup_inputs(seed: int = 0) -> dict:
    arg_keys = jax.random.split(jax.random.key(seed), 6)
    queries = draw_queries(jax.random.fold_in(arg_keys[5], 71), 0)
    probes = draw_probes(jax.random.fold_in(arg_keys[5], 71), 0)
    keys = draw_keys(jax.random.fold_in(arg_keys[5], 71), 0)
    values = gaussian(arg_keys[3], (N_SEQ, MEMORY, D), 1.0, 6.0, ((0, 4), (1, 8)))
    w_out = gaussian(arg_keys[4], (D, D), 0.13, 0.75, ((0, 8), (1, 4)))
    return dict(queries=queries, probes=probes, keys=keys, values=values, w_out=w_out)


def attend_head(inputs):
    head_query, head_probe, head_keys, head_values = inputs
    scaling = DH ** -0.5
    chosen_keys = head_keys[head_probe].astype(jnp.float32)
    chosen_values = head_values[head_probe].astype(jnp.float32)
    scores = jnp.einsum("qd,qtkd->qtk", head_query.astype(jnp.float32), chosen_keys) * scaling
    row_top = jnp.max(scores, axis=(1, 2), keepdims=True)
    weights = jnp.exp(scores - row_top)
    totals = jnp.sum(weights, axis=(1, 2))
    rounded = lax.optimization_barrier(weights.astype(jnp.bfloat16)).astype(jnp.float32)
    numerator = jnp.einsum("qtk,qtkd->qd", rounded, chosen_values)
    return numerator / totals[:, None]


def attend_group(inputs):
    group_query, group_probe, group_keys, group_values = inputs
    group_rows = group_query.shape[0]
    block_count = group_keys.shape[0] // BLOCK
    query_heads = jnp.transpose(group_query.reshape(group_rows, H, DH), (1, 0, 2))
    probe_heads = jnp.transpose(group_probe, (1, 0, 2))
    key_heads = jnp.transpose(group_keys.reshape(block_count, BLOCK, H, DH), (2, 0, 1, 3))
    value_heads = jnp.transpose(group_values.reshape(block_count, BLOCK, H, DH), (2, 0, 1, 3))
    result = lax.map(attend_head, (query_heads, probe_heads, key_heads, value_heads))
    return jnp.transpose(result, (1, 0, 2)).reshape(group_rows, H * DH).astype(jnp.bfloat16)


def reference(queries, probes, keys, values, w_out):
    group_rows = Q_DEV * N_MEM
    attended = lax.map(attend_group, (queries.reshape(N_SEQ, group_rows, D), probes.reshape(N_SEQ, group_rows, H, TOPB), keys, values))
    attended = attended.reshape(N_SEQ * group_rows, D)
    return jnp.dot(attended, w_out, preferred_element_type=jnp.float32).astype(jnp.bfloat16)
```

```python
import functools

import jax
import jax.numpy as jnp
from jax import lax
from jax.experimental import pallas as pl
from jax.experimental.pallas import tpu as pltpu
from jax.sharding import PartitionSpec as P

H = 64
DH = 128
BLOCK = 256
LOW = -1e30
DELAY = 1
MESH = pl.DeviceIdType.MESH
F32 = jnp.float32
BF16 = jnp.bfloat16


def kernel(
    n, ns, q_ref, bias_ref, k_ref, v_ref, w_ref, out_ref,
    qg, kbuf, vbuf, wbuf, own, own_st, sib, sib_st, chn, chn_st, gat, part, psib, pchn, obuf,
    kv_sem, w_sem, q_sem, qs_send, qs_recv, rl_send, rl_recv, as_send, as_recv, ac_send, ac_recv,
    g_send, g_recv, bs_send, bs_recv, bc_send, bc_recv, o_send, o_recv,
):
    nc = n // 2
    slots = kbuf.shape[0]
    rows_here, _ = q_ref.shape
    rows = qg.shape[1]
    wide = qg.shape[2]
    feats = wide // 2
    heads = feats // DH
    keys = kbuf.shape[1]
    blocks = keys // BLOCK
    cols = wbuf.shape[1]
    st_rows = own_st.shape[2]
    s = lax.axis_index("seq")
    me = lax.axis_index("mem")
    p = me // 2
    c = me % 2
    twin = (s, p * 2 + 1 - c)

    def peer(d):
        return (s, ((p + d) % nc) * 2 + c)

    def across(d):
        return ((s + d) % ns, me)

    def turn(i):
        return (i % 2) * (nc - 1 - i // 2) + (1 - i % 2) * (i // 2)

    def remote(src, dst, send, recv, to):
        return pltpu.make_async_remote_copy(
            src_ref=src, dst_ref=dst, send_sem=send, recv_sem=recv, device_id=to, device_id_type=MESH
        )

    def span(i, size):
        return pl.ds(pl.multiple_of(i * size, size), size)

    def key_copies(i):
        at = turn(i)
        slot = i % slots
        return (
            pltpu.make_async_copy(k_ref.at[0, :, span(at, wide)], kbuf.at[slot], kv_sem.at[slot, 0]),
            pltpu.make_async_copy(v_ref.at[0, :, span(at, wide)], vbuf.at[slot], kv_sem.at[slot, 1]),
        )

    def own_query(at):
        return pltpu.make_async_copy(
            q_ref.at[:, span(at, wide)], qg.at[at, span(me, rows_here), :], q_sem.at[at]
        )

    def query_send(at, d):
        return remote(
            q_ref.at[:, span(at, wide)], qg.at[at, span(me, rows_here), :],
            qs_send.at[at, d], qs_recv.at[at, d], peer(d),
        )

    def query_twin(at):
        return remote(
            q_ref.at[:, span(at, wide)], qg.at[at, span(me, rows_here), :],
            rl_send.at[at, 0], rl_recv.at[at, 0], twin,
        )

    def query_relay(at, d):
        source = ((p + nc - d) % nc) * 2 + c
        piece = qg.at[at, span(source, rows_here), :]
        return remote(piece, piece, rl_send.at[at, d], rl_recv.at[at, d], twin)

    weight_copy = pltpu.make_async_copy(w_ref, wbuf, w_sem.at[0])

    barrier = pltpu.get_barrier_semaphore()
    for d in range(1, nc):
        pl.semaphore_signal(barrier, inc=1, device_id=peer(d), device_id_type=MESH)
    for d in range(1, ns):
        pl.semaphore_signal(barrier, inc=1, device_id=across(d), device_id_type=MESH)
    pl.semaphore_signal(barrier, inc=1, device_id=twin, device_id_type=MESH)
    pl.semaphore_wait(barrier, nc + ns - 1)

    def start_queries(i, carry):
        at = turn(i)
        for d in range(1, nc):
            query_send(at, d).start()
        query_twin(at).start()
        own_query(at).start()
        return carry

    lax.fori_loop(0, nc, start_queries, 0)
    for i in range(slots):
        for copy in key_copies(i):
            copy.start()
    weight_copy.start()

    lane = lax.broadcasted_iota(jnp.int32, (rows, 128), 1)

    def twin_send(at):
        return (
            remote(own.at[at, 1 - c], sib.at[at], as_send.at[at, 0], as_recv.at[at, 0], twin),
            remote(own_st.at[at, 1 - c], sib_st.at[at], as_send.at[at, 1], as_recv.at[at, 1], twin),
        )

    def attend(i):
        at = turn(i)
        slot = i % slots
        for d in range(1, nc):
            query_send(at, d).wait_recv()
            query_relay(at, d).start()
        for copy in key_copies(i):
            copy.wait()
        own_query(at).wait()
        query_twin(at).wait_recv()
        for d in range(1, nc):
            query_relay(at, d).wait_recv()
        for side in range(2):
            stats = jnp.zeros((rows, 128), F32)
            for head in range(heads):
                lo = side * feats + head * DH
                query = qg[at, :, lo : lo + DH]
                scores = lax.dot_general(
                    query, kbuf[slot, :, lo : lo + DH], (((1,), (1,)), ((), ())), preferred_element_type=F32
                ) * (DH ** -0.5)
                pieces = []
                for b in range(blocks):
                    at_lane = (side * heads + head) * blocks + b
                    pieces.append(
                        scores[:, b * BLOCK : (b + 1) * BLOCK] + bias_ref[at, :, at_lane : at_lane + 1]
                    )
                top = functools.reduce(
                    jnp.maximum, [jnp.max(piece, axis=1, keepdims=True) for piece in pieces]
                )
                weights = jnp.concatenate([jnp.exp(piece - top) for piece in pieces], axis=1)
                total = jnp.sum(weights, axis=1, keepdims=True)
                numer = jnp.dot(
                    weights.astype(BF16), vbuf[slot, :, lo : lo + DH], preferred_element_type=F32
                )
                own[at, side, :, head * DH : (head + 1) * DH] = numer.astype(BF16)
                stats = jnp.where(lane == head, top, stats)
                stats = jnp.where(lane == heads + head, total, stats)
            own_st[at, side] = stats.T[:st_rows]
        for copy in twin_send(at):
            copy.start()

        @pl.when(i + slots < nc)
        def _():
            for copy in key_copies(i + slots):
                copy.start()

    def hop(at, nums, sts, send, recv):
        def pair(slot, to):
            made = []
            for x, (mine, theirs) in enumerate(zip(nums, sts)):
                made.append(remote(mine.at[at, c], theirs.at[slot], send.at[at, x], recv.at[slot, x], to))
            return made

        return pair

    def a_pair(at):
        return hop(at, (own, own_st), (chn, chn_st), ac_send, ac_recv)

    def b_pair(at):
        return hop(at, (part,), (pchn,), bc_send, bc_recv)

    def move(at, maker, begin):
        @pl.when(at > p)
        def _():
            for copy in maker(at)(at, (s, (p + 1) * 2 + c)):
                if begin:
                    copy.start()
                else:
                    copy.wait_send()

        @pl.when((at < p) & ((at != p - 1) | (at == 0)))
        def _():
            for copy in maker(at)(at, (s, (p - 1) * 2 + c)):
                if begin:
                    copy.start()
                else:
                    copy.wait_send()

        @pl.when((at < p) & (at == p - 1) & (at > 0))
        def _():
            for copy in maker(at)(nc, (s, (p - 1) * 2 + c)):
                if begin:
                    copy.start()
                else:
                    copy.wait_send()

    def arrive(at, maker, slot):
        for copy in maker(at)(slot, twin):
            copy.wait_recv()

    def cases(at, body):
        ends = ((at > p) & (p == 0)) | ((at < p) & (p == nc - 1))
        both = (at == p) & (p > 0) & (p < nc - 1)

        @pl.when(ends)
        def _():
            body(0)

        @pl.when(jnp.logical_not(ends | both))
        def _():
            body(1)

        @pl.when(both)
        def _():
            body(2)

    def merge(at):
        for copy in twin_send(at):
            copy.wait_recv()

        def body(count):
            sources = [(own.at[at, c], own_st.at[at, c]), (sib.at[at], sib_st.at[at])]
            for slot in (at, nc)[:count]:
                arrive(at, a_pair, slot)
                sources.append((chn.at[slot], chn_st.at[slot]))
            tops = [st[:heads] for _, st in sources]
            sums = [st[heads : 2 * heads] for _, st in sources]
            top = functools.reduce(jnp.maximum, tops)
            scales = [jnp.exp(t - top) for t in tops]
            total = functools.reduce(jnp.add, [e * t for e, t in zip(scales, sums)])
            done = at == p
            factor = jnp.where(done, 1.0 / total, jnp.ones_like(total))
            scales = [e * factor for e in scales]
            filler = jnp.zeros((128 - heads * len(scales), rows), F32)
            lanes = jnp.concatenate(scales + [filler], axis=0).T
            for head in range(heads):
                cut = slice(head * DH, (head + 1) * DH)
                value = functools.reduce(
                    jnp.add,
                    [
                        num[:, cut].astype(F32) * lanes[:, x * heads + head : x * heads + head + 1]
                        for x, (num, _) in enumerate(sources)
                    ],
                )
                own[at, c, :, cut] = value.astype(BF16)
            own_st[at, c, :heads] = top
            own_st[at, c, heads : 2 * heads] = total

        cases(at, body)
        move(at, a_pair, True)

    def attention(i, carry):
        @pl.when(i < nc)
        def _():
            attend(i)

        @pl.when(i >= DELAY)
        def _():
            merge(turn(i - DELAY))

        return carry

    lax.fori_loop(0, nc + DELAY, attention, 0)

    def spread(d):
        return remote(own.at[p, c], gat.at[s], g_send.at[d], g_recv.at[d], across(d))

    for d in range(1, ns):
        spread(d).start()
    gat[s] = own[p, c]
    weight_copy.wait()
    for d in range(1, ns):
        spread(d).wait_recv()

    def part_send(at):
        return remote(part.at[at, 1 - c], psib.at[at], bs_send.at[at], bs_recv.at[at], twin)

    def project(i):
        at = turn(i)
        for side in range(2):
            piece = gat[:, pl.ds(pl.multiple_of((at * 2 + side) * rows_here, rows_here), rows_here), :]
            piece = piece.reshape(ns * rows_here, feats)
            part[at, side] = jnp.dot(piece, wbuf[...], preferred_element_type=F32).astype(BF16)
        part_send(at).start()

    def add(at):
        part_send(at).wait_recv()

        def body(count):
            sources = [part.at[at, c], psib.at[at]]
            for slot in (at, nc)[:count]:
                arrive(at, b_pair, slot)
                sources.append(pchn.at[slot])
            step = 512
            for lo in range(0, cols, step):
                value = functools.reduce(jnp.add, [x[:, lo : lo + step].astype(F32) for x in sources])
                part[at, c, :, lo : lo + step] = value.astype(BF16)

        cases(at, body)
        move(at, b_pair, True)

    def projection(i, carry):
        @pl.when(i < nc)
        def _():
            project(i)

        @pl.when(i >= DELAY)
        def _():
            add(turn(i - DELAY))

        return carry

    lax.fori_loop(0, nc + DELAY, projection, 0)

    def deliver(d):
        to = (s + d) % ns
        return remote(
            part.at[p, c, span(to, rows_here), :], obuf.at[s], o_send.at[d], o_recv.at[d], across(d)
        )

    for d in range(1, ns):
        deliver(d).start()
    obuf[s] = part[p, c, span(s, rows_here), :]

    def drain(i, carry):
        for d in range(1, nc):
            query_send(i, d).wait_send()
            query_relay(i, d).wait_send()
        query_twin(i).wait_send()
        for copy in twin_send(i):
            copy.wait_send()
        part_send(i).wait_send()
        move(i, a_pair, False)
        move(i, b_pair, False)
        return carry

    lax.fori_loop(0, nc, drain, 0)
    for d in range(1, ns):
        spread(d).wait_send()
        deliver(d).wait_recv()
    for t in range(ns):
        out_ref[:, t * cols : (t + 1) * cols] = obuf[t]
    for d in range(1, ns):
        deliver(d).wait_send()


def shards(n, ns, queries, probes, keys, values, w_out):
    nc = n // 2
    rows_here, width = queries.shape
    rows = probes.shape[0]
    local_keys = keys.shape[1]
    local_blocks = local_keys // BLOCK
    feats, cols = w_out.shape
    wide = 2 * feats
    heads = feats // DH
    st_rows = max(8, 2 * heads)
    slots = min(nc, 4)
    block_ids = lax.axis_index("mem") * local_blocks + jnp.arange(local_blocks, dtype=jnp.int32)
    probed = jnp.any(probes[:, :, :, None] == block_ids[None, None, None, :], axis=2)
    bias = jnp.where(probed, 0.0, LOW).astype(F32).reshape(rows, nc, 2 * heads * local_blocks)
    bias = jnp.transpose(bias, (1, 0, 2))
    dma = pltpu.SemaphoreType.DMA
    vm = pltpu.VMEM
    flops = 4 * rows * width * local_keys + 2 * ns * rows * feats * cols
    return pl.pallas_call(
        functools.partial(kernel, n, ns),
        out_shape=jax.ShapeDtypeStruct((rows_here, ns * cols), BF16),
        in_specs=[
            pl.BlockSpec(memory_space=pl.ANY),
            pl.BlockSpec(memory_space=pltpu.VMEM),
            pl.BlockSpec(memory_space=pl.ANY),
            pl.BlockSpec(memory_space=pl.ANY),
            pl.BlockSpec(memory_space=pl.ANY),
        ],
        out_specs=pl.BlockSpec(memory_space=pltpu.VMEM),
        scratch_shapes=[
            vm((nc, rows, wide), BF16),
            vm((slots, local_keys, wide), BF16),
            vm((slots, local_keys, wide), BF16),
            vm((feats, cols), BF16),
            vm((nc, 2, rows, feats), BF16),
            vm((nc, 2, st_rows, rows), F32),
            vm((nc, rows, feats), BF16),
            vm((nc, st_rows, rows), F32),
            vm((nc + 1, rows, feats), BF16),
            vm((nc + 1, st_rows, rows), F32),
            vm((ns, rows, feats), BF16),
            vm((nc, 2, ns * rows_here, cols), BF16),
            vm((nc, ns * rows_here, cols), BF16),
            vm((nc + 1, ns * rows_here, cols), BF16),
            vm((ns, rows_here, cols), BF16),
            dma((slots, 2)),
            dma((1,)),
            dma((nc,)),
            dma((nc, nc)),
            dma((nc, nc)),
            dma((nc, nc)),
            dma((nc, nc)),
            dma((nc, 2)),
            dma((nc, 2)),
            dma((nc, 2)),
            dma((nc + 1, 2)),
            dma((ns,)),
            dma((ns,)),
            dma((nc,)),
            dma((nc,)),
            dma((nc, 1)),
            dma((nc + 1, 1)),
            dma((ns,)),
            dma((ns,)),
        ],
        compiler_params=pltpu.CompilerParams(
            collective_id=0, has_side_effects=True, vmem_limit_bytes=60 * 1024 * 1024
        ),
        cost_estimate=pl.CostEstimate(
            flops=flops, bytes_accessed=4 * local_keys * width + 2 * feats * cols,
            transcendentals=rows * H * local_keys,
        ),
    )(queries, bias, keys, values, w_out)


def solution(mesh):
    placed = (
        P(("seq", "mem"), None),
        P("seq", None, None),
        P("seq", "mem", None),
        P("seq", "mem", None),
        P("mem", "seq"),
    )
    body = functools.partial(shards, mesh.shape["mem"], mesh.shape["seq"])
    return jax.shard_map(
        body, mesh=mesh, in_specs=placed, out_specs=P(("seq", "mem"), None), check_vma=False
    )
```

```python
import functools

import jax
import jax.numpy as jnp
from jax import lax
from jax.experimental import pallas as pl
from jax.experimental.pallas import tpu as pltpu
from jax.sharding import PartitionSpec as P

H = 64
DH = 128
BLOCK = 256
LOW = -1e30
RATE = DH ** -0.5 * 1.4426950408889634
MESH = pl.DeviceIdType.MESH
F32 = jnp.float32
BF16 = jnp.bfloat16


def kernel(
    n, ns, q_ref, bias_ref, k_ref, v_ref, w_ref, out_ref,
    qg, kbuf, vbuf, wbuf, own, own_st, sib, sib_st, chn, chn_st, gat, part, psib, pchn, obuf,
    kv_sem, w_sem, q_sem, qs_send, qs_recv, rl_send, rl_recv, as_send, as_recv, ac_send, ac_recv,
    g_send, g_recv, bs_send, bs_recv, bc_send, bc_recv, o_send, o_recv,
):
    nc = n // 2
    slots = kbuf.shape[0]
    rows_here, _ = q_ref.shape
    rows = qg.shape[1]
    wide = qg.shape[2]
    feats = wide // 2
    heads = feats // DH
    keys = kbuf.shape[1]
    blocks = keys // BLOCK
    cols = wbuf.shape[1]
    st_rows = own_st.shape[2]
    s = lax.axis_index("seq")
    me = lax.axis_index("mem")
    p = me // 2
    c = me % 2
    twin = (s, p * 2 + 1 - c)

    def peer(d):
        return (s, ((p + d) % nc) * 2 + c)

    def across(d):
        return ((s + d) % ns, me)

    def turn(i):
        return (i % 2) * (nc - 1 - i // 2) + (1 - i % 2) * (i // 2)

    def remote(src, dst, send, recv, to):
        return pltpu.make_async_remote_copy(
            src_ref=src, dst_ref=dst, send_sem=send, recv_sem=recv, device_id=to, device_id_type=MESH
        )

    def span(i, size):
        return pl.ds(pl.multiple_of(i * size, size), size)

    def key_copies(i):
        at = turn(i)
        slot = i % slots
        return (
            pltpu.make_async_copy(k_ref.at[0, :, span(at, wide)], kbuf.at[slot], kv_sem.at[slot, 0]),
            pltpu.make_async_copy(v_ref.at[0, :, span(at, wide)], vbuf.at[slot], kv_sem.at[slot, 1]),
        )

    def own_query(at):
        return pltpu.make_async_copy(
            q_ref.at[:, span(at, wide)], qg.at[at, span(me, rows_here), :], q_sem.at[at]
        )

    def query_send(at, d):
        return remote(
            q_ref.at[:, span(at, wide)], qg.at[at, span(me, rows_here), :],
            qs_send.at[at, d], qs_recv.at[at, d], peer(d),
        )

    def query_twin(at):
        return remote(
            q_ref.at[:, span(at, wide)], qg.at[at, span(me, rows_here), :],
            rl_send.at[at, 0], rl_recv.at[at, 0], twin,
        )

    def query_relay(at, d):
        source = ((p + nc - d) % nc) * 2 + c
        piece = qg.at[at, span(source, rows_here), :]
        return remote(piece, piece, rl_send.at[at, d], rl_recv.at[at, d], twin)

    weight_copy = pltpu.make_async_copy(w_ref, wbuf, w_sem.at[0])

    barrier = pltpu.get_barrier_semaphore()
    for d in range(1, nc):
        pl.semaphore_signal(barrier, inc=1, device_id=peer(d), device_id_type=MESH)
    for d in range(1, ns):
        pl.semaphore_signal(barrier, inc=1, device_id=across(d), device_id_type=MESH)
    pl.semaphore_signal(barrier, inc=1, device_id=twin, device_id_type=MESH)
    pl.semaphore_wait(barrier, nc + ns - 1)

    def start_queries(i, carry):
        at = turn(i)
        for d in range(1, nc):
            query_send(at, d).start()
        query_twin(at).start()
        own_query(at).start()
        return carry

    lax.fori_loop(0, nc, start_queries, 0)
    for i in range(slots):
        for copy in key_copies(i):
            copy.start()
    weight_copy.start()

    lane = lax.broadcasted_iota(jnp.int32, (rows, 128), 1)

    def twin_send(at):
        return (
            remote(own.at[at, 1 - c], sib.at[at], as_send.at[at, 0], as_recv.at[at, 0], twin),
            remote(own_st.at[at, 1 - c], sib_st.at[at], as_send.at[at, 1], as_recv.at[at, 1], twin),
        )

    def attend(i):
        at = turn(i)
        slot = i % slots
        for d in range(1, nc):
            query_send(at, d).wait_recv()
            query_relay(at, d).start()
        for copy in key_copies(i):
            copy.wait()
        own_query(at).wait()
        query_twin(at).wait_recv()
        for d in range(1, nc):
            query_relay(at, d).wait_recv()
        for side in range(2):
            stats = jnp.zeros((rows, 128), F32)
            for head in range(heads):
                lo = side * feats + head * DH
                query = qg[at, :, lo : lo + DH]
                scores = lax.dot_general(
                    query, kbuf[slot, :, lo : lo + DH], (((1,), (1,)), ((), ())), preferred_element_type=F32
                )
                pieces = []
                for b in range(blocks):
                    at_lane = (side * heads + head) * blocks + b
                    pieces.append(
                        scores[:, b * BLOCK : (b + 1) * BLOCK] + bias_ref[at, :, at_lane : at_lane + 1]
                    )
                top = functools.reduce(
                    jnp.maximum, [jnp.max(piece, axis=1, keepdims=True) for piece in pieces]
                )
                weights = jnp.concatenate([jnp.exp2((piece - top) * RATE) for piece in pieces], axis=1)
                total = jnp.sum(weights, axis=1, keepdims=True)
                numer = jnp.dot(
                    weights.astype(BF16), vbuf[slot, :, lo : lo + DH], preferred_element_type=F32
                )
                own[at, side, :, head * DH : (head + 1) * DH] = numer.astype(BF16)
                stats = jnp.where(lane == head, top, stats)
                stats = jnp.where(lane == heads + head, total, stats)
            own_st[at, side] = stats.T[:st_rows]
        for copy in twin_send(at):
            copy.start()

        @pl.when(i + slots < nc)
        def _():
            for copy in key_copies(i + slots):
                copy.start()

    def hop(at, nums, sts, send, recv):
        def pair(slot, to):
            made = []
            for x, (mine, theirs) in enumerate(zip(nums, sts)):
                made.append(remote(mine.at[at, c], theirs.at[slot], send.at[at, x], recv.at[slot, x], to))
            return made

        return pair

    def a_pair(at):
        return hop(at, (own, own_st), (chn, chn_st), ac_send, ac_recv)

    def b_pair(at):
        return hop(at, (part,), (pchn,), bc_send, bc_recv)

    def move(at, maker, begin):
        @pl.when(at > p)
        def _():
            for copy in maker(at)(at, (s, (p + 1) * 2 + c)):
                if begin:
                    copy.start()
                else:
                    copy.wait_send()

        @pl.when((at < p) & ((at != p - 1) | (at == 0)))
        def _():
            for copy in maker(at)(at, (s, (p - 1) * 2 + c)):
                if begin:
                    copy.start()
                else:
                    copy.wait_send()

        @pl.when((at < p) & (at == p - 1) & (at > 0))
        def _():
            for copy in maker(at)(nc, (s, (p - 1) * 2 + c)):
                if begin:
                    copy.start()
                else:
                    copy.wait_send()

    def arrive(at, maker, slot):
        for copy in maker(at)(slot, twin):
            copy.wait_recv()

    def cases(at, body):
        ends = ((at > p) & (p == 0)) | ((at < p) & (p == nc - 1))
        both = (at == p) & (p > 0) & (p < nc - 1)

        @pl.when(ends)
        def _():
            body(0)

        @pl.when(jnp.logical_not(ends | both))
        def _():
            body(1)

        @pl.when(both)
        def _():
            body(2)

    def merge(at):
        for copy in twin_send(at):
            copy.wait_recv()

        def body(count):
            sources = [(own.at[at, c], own_st.at[at, c]), (sib.at[at], sib_st.at[at])]
            for slot in (at, nc)[:count]:
                arrive(at, a_pair, slot)
                sources.append((chn.at[slot], chn_st.at[slot]))
            tops = [st[:heads] for _, st in sources]
            sums = [st[heads : 2 * heads] for _, st in sources]
            top = functools.reduce(jnp.maximum, tops)
            scales = [jnp.exp2((t - top) * RATE) for t in tops]
            total = functools.reduce(jnp.add, [e * t for e, t in zip(scales, sums)])
            done = at == p
            factor = jnp.where(done, 1.0 / total, jnp.ones_like(total))
            scales = [e * factor for e in scales]
            filler = jnp.zeros((128 - heads * len(scales), rows), F32)
            lanes = jnp.concatenate(scales + [filler], axis=0).T
            for head in range(heads):
                cut = slice(head * DH, (head + 1) * DH)
                value = functools.reduce(
                    jnp.add,
                    [
                        num[:, cut].astype(F32) * lanes[:, x * heads + head : x * heads + head + 1]
                        for x, (num, _) in enumerate(sources)
                    ],
                )
                own[at, c, :, cut] = value.astype(BF16)
            own_st[at, c, :heads] = top
            own_st[at, c, heads : 2 * heads] = total

        cases(at, body)
        move(at, a_pair, True)

    turns = nc + nc - nc // 2

    def advance(i, join):
        late = i // nc
        k = (1 - late) * (i // 2) + late * (i - nc + nc // 2)

        def one(side, carry):
            dest = (1 - side) * (nc - 1 - k + p) + side * (k - nc + 1 + p)
            wanted = ((side == 0) & (dest < nc)) | ((side == 1) & (dest >= 0) & (dest < p))

            @pl.when(wanted)
            def _():
                join(dest)

            return carry

        @pl.when((late == 1) | (i % 2 == 1))
        def _():
            lax.fori_loop(0, 2, one, 0)

    def attention(i, carry):
        @pl.when(i < nc)
        def _():
            attend(i)

        advance(i, merge)
        return carry

    lax.fori_loop(0, turns, attention, 0)

    def spread(d):
        return remote(own.at[p, c], gat.at[s], g_send.at[d], g_recv.at[d], across(d))

    for d in range(1, ns):
        spread(d).start()
    gat[s] = own[p, c]
    weight_copy.wait()
    for d in range(1, ns):
        spread(d).wait_recv()

    def part_send(at):
        return remote(part.at[at, 1 - c], psib.at[at], bs_send.at[at], bs_recv.at[at], twin)

    def project(i):
        at = turn(i)
        for side in range(2):
            piece = gat[:, pl.ds(pl.multiple_of((at * 2 + side) * rows_here, rows_here), rows_here), :]
            piece = piece.reshape(ns * rows_here, feats)
            part[at, side] = jnp.dot(piece, wbuf[...], preferred_element_type=F32).astype(BF16)
        part_send(at).start()

    def add(at):
        part_send(at).wait_recv()

        def body(count):
            sources = [part.at[at, c], psib.at[at]]
            for slot in (at, nc)[:count]:
                arrive(at, b_pair, slot)
                sources.append(pchn.at[slot])
            step = 512
            for lo in range(0, cols, step):
                value = functools.reduce(jnp.add, [x[:, lo : lo + step].astype(F32) for x in sources])
                part[at, c, :, lo : lo + step] = value.astype(BF16)

        cases(at, body)
        move(at, b_pair, True)

    def projection(i, carry):
        @pl.when(i < nc)
        def _():
            project(i)

        advance(i, add)
        return carry

    lax.fori_loop(0, turns, projection, 0)

    def deliver(d):
        to = (s + d) % ns
        return remote(
            part.at[p, c, span(to, rows_here), :], obuf.at[s], o_send.at[d], o_recv.at[d], across(d)
        )

    for d in range(1, ns):
        deliver(d).start()
    obuf[s] = part[p, c, span(s, rows_here), :]

    def drain(i, carry):
        for d in range(1, nc):
            query_send(i, d).wait_send()
            query_relay(i, d).wait_send()
        query_twin(i).wait_send()
        for copy in twin_send(i):
            copy.wait_send()
        part_send(i).wait_send()
        move(i, a_pair, False)
        move(i, b_pair, False)
        return carry

    lax.fori_loop(0, nc, drain, 0)
    for d in range(1, ns):
        spread(d).wait_send()
        deliver(d).wait_recv()
    for t in range(ns):
        out_ref[:, t * cols : (t + 1) * cols] = obuf[t]
    for d in range(1, ns):
        deliver(d).wait_send()


def shards(n, ns, queries, probes, keys, values, w_out):
    nc = n // 2
    rows_here, width = queries.shape
    rows = probes.shape[0]
    local_keys = keys.shape[1]
    local_blocks = local_keys // BLOCK
    feats, cols = w_out.shape
    wide = 2 * feats
    heads = feats // DH
    st_rows = max(8, 2 * heads)
    slots = min(nc, 4)
    block_ids = lax.axis_index("mem") * local_blocks + jnp.arange(local_blocks, dtype=jnp.int32)
    probed = jnp.any(probes[:, :, :, None] == block_ids[None, None, None, :], axis=2)
    bias = jnp.where(probed, 0.0, LOW).astype(F32).reshape(rows, nc, 2 * heads * local_blocks)
    bias = jnp.transpose(bias, (1, 0, 2))
    dma = pltpu.SemaphoreType.DMA
    vm = pltpu.VMEM
    flops = 4 * rows * width * local_keys + 2 * ns * rows * feats * cols
    return pl.pallas_call(
        functools.partial(kernel, n, ns),
        out_shape=jax.ShapeDtypeStruct((rows_here, ns * cols), BF16),
        in_specs=[
            pl.BlockSpec(memory_space=pl.ANY),
            pl.BlockSpec(memory_space=pltpu.VMEM),
            pl.BlockSpec(memory_space=pl.ANY),
            pl.BlockSpec(memory_space=pl.ANY),
            pl.BlockSpec(memory_space=pl.ANY),
        ],
        out_specs=pl.BlockSpec(memory_space=pltpu.VMEM),
        scratch_shapes=[
            vm((nc, rows, wide), BF16),
            vm((slots, local_keys, wide), BF16),
            vm((slots, local_keys, wide), BF16),
            vm((feats, cols), BF16),
            vm((nc, 2, rows, feats), BF16),
            vm((nc, 2, st_rows, rows), F32),
            vm((nc, rows, feats), BF16),
            vm((nc, st_rows, rows), F32),
            vm((nc + 1, rows, feats), BF16),
            vm((nc + 1, st_rows, rows), F32),
            vm((ns, rows, feats), BF16),
            vm((nc, 2, ns * rows_here, cols), BF16),
            vm((nc, ns * rows_here, cols), BF16),
            vm((nc + 1, ns * rows_here, cols), BF16),
            vm((ns, rows_here, cols), BF16),
            dma((slots, 2)),
            dma((1,)),
            dma((nc,)),
            dma((nc, nc)),
            dma((nc, nc)),
            dma((nc, nc)),
            dma((nc, nc)),
            dma((nc, 2)),
            dma((nc, 2)),
            dma((nc, 2)),
            dma((nc + 1, 2)),
            dma((ns,)),
            dma((ns,)),
            dma((nc,)),
            dma((nc,)),
            dma((nc, 1)),
            dma((nc + 1, 1)),
            dma((ns,)),
            dma((ns,)),
        ],
        compiler_params=pltpu.CompilerParams(
            collective_id=0, has_side_effects=True, vmem_limit_bytes=60 * 1024 * 1024
        ),
        cost_estimate=pl.CostEstimate(
            flops=flops, bytes_accessed=4 * local_keys * width + 2 * feats * cols,
            transcendentals=rows * H * local_keys,
        ),
    )(queries, bias, keys, values, w_out)


def solution(mesh):
    placed = (
        P(("seq", "mem"), None),
        P("seq", None, None),
        P("seq", "mem", None),
        P("seq", "mem", None),
        P("mem", "seq"),
    )
    body = functools.partial(shards, mesh.shape["mem"], mesh.shape["seq"])
    return jax.shard_map(
        body, mesh=mesh, in_specs=placed, out_specs=P(("seq", "mem"), None), check_vma=False
    )
```

```python
import functools

import jax
import jax.numpy as jnp
from jax import lax
from jax.experimental import pallas as pl
from jax.experimental.pallas import tpu as pltpu
from jax.sharding import PartitionSpec as P

H = 64
DH = 128
BLOCK = 256
LOW = -1e30
RATE = DH ** -0.5 * 1.4426950408889634
MESH = pl.DeviceIdType.MESH
F32 = jnp.float32
BF16 = jnp.bfloat16


def kernel(
    n, ns, q_ref, bias_ref, k_ref, v_ref, w_ref, out_ref,
    qg, kbuf, vbuf, wbuf, own, own_st, sib, sib_st, chn, chn_st, gat, part, psib, pchn, obuf,
    kv_sem, w_sem, q_sem, qs_send, qs_recv, rl_send, rl_recv, as_send, as_recv, ac_send, ac_recv,
    g_send, g_recv, bs_send, bs_recv, bc_send, bc_recv, o_send, o_recv,
):
    nc = n // 2
    slots = kbuf.shape[0]
    rows_here, _ = q_ref.shape
    rows = qg.shape[1]
    wide = qg.shape[2]
    feats = wide // 2
    heads = feats // DH
    half_heads = heads // 2
    half_feats = feats // 2
    keys = kbuf.shape[1]
    blocks = keys // BLOCK
    cols = wbuf.shape[1]
    half_cols = cols // 2
    st_rows = own_st.shape[2]
    s = lax.axis_index("seq")
    me = lax.axis_index("mem")
    p = me // 2
    c = me % 2
    twin = (s, p * 2 + 1 - c)

    def peer(d):
        return (s, ((p + d) % nc) * 2 + c)

    def across(d):
        return ((s + d) % ns, me)

    def turn(i):
        return (i % 2) * (nc - 1 - i // 2) + (1 - i % 2) * (i // 2)

    def remote(src, dst, send, recv, to):
        return pltpu.make_async_remote_copy(
            src_ref=src, dst_ref=dst, send_sem=send, recv_sem=recv, device_id=to, device_id_type=MESH
        )

    def span(i, size):
        return pl.ds(pl.multiple_of(i * size, size), size)

    def key_copies(i):
        at = turn(i)
        slot = i % slots
        return (
            pltpu.make_async_copy(k_ref.at[0, :, span(at, wide)], kbuf.at[slot], kv_sem.at[slot, 0]),
            pltpu.make_async_copy(v_ref.at[0, :, span(at, wide)], vbuf.at[slot], kv_sem.at[slot, 1]),
        )

    def own_query(at):
        return pltpu.make_async_copy(
            q_ref.at[:, span(at, wide)], qg.at[at, span(me, rows_here), :], q_sem.at[at]
        )

    def query_send(at, d):
        return remote(
            q_ref.at[:, span(at, wide)], qg.at[at, span(me, rows_here), :],
            qs_send.at[at, d], qs_recv.at[at, d], peer(d),
        )

    def query_twin(at):
        return remote(
            q_ref.at[:, span(at, wide)], qg.at[at, span(me, rows_here), :],
            rl_send.at[at, 0], rl_recv.at[at, 0], twin,
        )

    def query_relay(at, d):
        source = ((p + nc - d) % nc) * 2 + c
        piece = qg.at[at, span(source, rows_here), :]
        return remote(piece, piece, rl_send.at[at, d], rl_recv.at[at, d], twin)

    weight_copy = pltpu.make_async_copy(w_ref, wbuf, w_sem.at[0])

    barrier = pltpu.get_barrier_semaphore()
    for d in range(1, nc):
        pl.semaphore_signal(barrier, inc=1, device_id=peer(d), device_id_type=MESH)
    for d in range(1, ns):
        pl.semaphore_signal(barrier, inc=1, device_id=across(d), device_id_type=MESH)
    pl.semaphore_signal(barrier, inc=1, device_id=twin, device_id_type=MESH)
    pl.semaphore_wait(barrier, nc + ns - 1)

    def start_queries(i, carry):
        at = turn(i)
        for d in range(1, nc):
            query_send(at, d).start()
        query_twin(at).start()
        own_query(at).start()
        return carry

    lax.fori_loop(0, nc, start_queries, 0)
    for i in range(slots):
        for copy in key_copies(i):
            copy.start()
    weight_copy.start()

    lane = lax.broadcasted_iota(jnp.int32, (rows, 128), 1)

    def twin_send(at):
        return (
            remote(own.at[at, 1 - c], sib.at[at], as_send.at[at, 0], as_recv.at[at, 0], twin),
            remote(own_st.at[at, 1 - c], sib_st.at[at], as_send.at[at, 1], as_recv.at[at, 1], twin),
        )

    def relay(at):
        for d in range(1, nc):
            query_send(at, d).wait_recv()
            query_relay(at, d).start()

    def attend(i):
        at = turn(i)
        slot = i % slots
        for copy in key_copies(i):
            copy.wait()
        own_query(at).wait()
        query_twin(at).wait_recv()
        for d in range(1, nc):
            query_relay(at, d).wait_recv()

        def raw(x):
            cut = slice(x * DH, (x + 1) * DH)
            return lax.dot_general(
                qg[at, :, cut], kbuf[slot, :, cut], (((1,), (1,)), ((), ())), preferred_element_type=F32
            )

        scores = raw(0)
        for side in range(2):
            stats = jnp.zeros((rows, 128), F32)
            for head in range(heads):
                x = side * heads + head
                later = raw(x + 1) if x + 1 < 2 * heads else None
                pieces = []
                for b in range(blocks):
                    lane_at = x * blocks + b
                    pieces.append(
                        scores[:, b * BLOCK : (b + 1) * BLOCK] + bias_ref[at, :, lane_at : lane_at + 1]
                    )
                top = functools.reduce(
                    jnp.maximum, [jnp.max(piece, axis=1, keepdims=True) for piece in pieces]
                )
                weights = jnp.concatenate([jnp.exp2((piece - top) * RATE) for piece in pieces], axis=1)
                total = jnp.sum(weights, axis=1, keepdims=True)
                numer = jnp.dot(
                    weights.astype(BF16), vbuf[slot, :, x * DH : (x + 1) * DH], preferred_element_type=F32
                )
                half, place = head // half_heads, head % half_heads
                own[at, side, half, :, place * DH : (place + 1) * DH] = numer.astype(BF16)
                stats = jnp.where(lane == head, top, stats)
                stats = jnp.where(lane == heads + head, total, stats)
                scores = later
            own_st[at, side] = stats.T[:st_rows]
            if side == 0:
                @pl.when(i + 1 < nc)
                def _():
                    relay(turn(i + 1))
        for copy in twin_send(at):
            copy.start()

        @pl.when(i + slots < nc)
        def _():
            for copy in key_copies(i + slots):
                copy.start()

    def a_pair(at, half, slot, to):
        made = [
            remote(own.at[at, c, half], chn.at[slot, half], ac_send.at[at, half], ac_recv.at[slot, half], to)
        ]
        if half == 0:
            made.append(remote(own_st.at[at, c], chn_st.at[slot], ac_send.at[at, 2], ac_recv.at[slot, 2], to))
        return made

    def b_pair(at, half, slot, to):
        return [
            remote(part.at[at, c, half], pchn.at[slot, half], bc_send.at[at, half], bc_recv.at[slot, half], to)
        ]

    def move(at, maker, half, begin):
        def go(slot, step):
            for copy in maker(at, half, slot, (s, (p + step) * 2 + c)):
                if begin:
                    copy.start()
                else:
                    copy.wait_send()

        @pl.when(at > p)
        def _():
            go(at, 1)

        @pl.when((at < p) & ((at != p - 1) | (at == 0)))
        def _():
            go(at, -1)

        @pl.when((at < p) & (at == p - 1) & (at > 0))
        def _():
            go(nc, -1)

    def arrive(at, maker, half, slot):
        for copy in maker(at, half, slot, twin):
            copy.wait_recv()

    def cases(at, body):
        ends = ((at > p) & (p == 0)) | ((at < p) & (p == nc - 1))
        both = (at == p) & (p > 0) & (p < nc - 1)

        @pl.when(ends)
        def _():
            body(0)

        @pl.when(jnp.logical_not(ends | both))
        def _():
            body(1)

        @pl.when(both)
        def _():
            body(2)

    def spread(d, half):
        return remote(
            own.at[p, c, half], gat.at[s, half], g_send.at[d, half], g_recv.at[d, half], across(d)
        )

    def merge(at):
        for copy in twin_send(at):
            copy.wait_recv()

        def body(count):
            places = (at, nc)[:count]
            sources = [(own.at[at, c], own_st.at[at, c]), (sib.at[at], sib_st.at[at])]
            for slot in places:
                arrive(at, a_pair, 0, slot)
                sources.append((chn.at[slot], chn_st.at[slot]))
            tops = [st[:heads] for _, st in sources]
            sums = [st[heads : 2 * heads] for _, st in sources]
            top = functools.reduce(jnp.maximum, tops)
            scales = [jnp.exp2((t - top) * RATE) for t in tops]
            total = functools.reduce(jnp.add, [e * t for e, t in zip(scales, sums)])
            done = at == p
            factor = jnp.where(done, 1.0 / total, jnp.ones_like(total))
            scales = [e * factor for e in scales]
            filler = jnp.zeros((128 - heads * len(scales), rows), F32)
            lanes = jnp.concatenate(scales + [filler], axis=0).T
            own_st[at, c, :heads] = top
            own_st[at, c, heads : 2 * heads] = total
            for half in range(2):
                if half == 1:
                    for slot in places:
                        arrive(at, a_pair, 1, slot)
                for place in range(half_heads):
                    cut = slice(place * DH, (place + 1) * DH)
                    head = half * half_heads + place
                    value = functools.reduce(
                        jnp.add,
                        [
                            num[half, :, cut].astype(F32) * lanes[:, x * heads + head : x * heads + head + 1]
                            for x, (num, _) in enumerate(sources)
                        ],
                    )
                    own[at, c, half, :, cut] = value.astype(BF16)
                if count < 2:
                    move(at, a_pair, half, True)
                if count > 0:
                    @pl.when(done)
                    def _():
                        for d in range(1, ns):
                            spread(d, half).start()
                        gat[s, half] = own[p, c, half]

        cases(at, body)

    turns = nc + nc - nc // 2

    def advance(i, join):
        late = i // nc
        k = (1 - late) * (i // 2) + late * (i - nc + nc // 2)

        def one(side, carry):
            dest = (1 - side) * (nc - 1 - k + p) + side * (k - nc + 1 + p)
            wanted = ((side == 0) & (dest < nc)) | ((side == 1) & (dest >= 0) & (dest < p))

            @pl.when(wanted)
            def _():
                join(dest)

            return carry

        @pl.when((late == 1) | (i % 2 == 1))
        def _():
            lax.fori_loop(0, 2, one, 0)

    def attention(i, carry):
        @pl.when(i < nc)
        def _():
            attend(i)

        advance(i, merge)
        return carry

    relay(turn(0))
    lax.fori_loop(0, turns, attention, 0)

    weight_copy.wait()
    for half in range(2):
        for d in range(1, ns):
            spread(d, half).wait_recv()

    def part_send(at):
        return remote(part.at[at, 1 - c], psib.at[at], bs_send.at[at], bs_recv.at[at], twin)

    def project(i):
        at = turn(i)
        mine = pl.ds(pl.multiple_of(at * 2 * rows_here, 2 * rows_here), 2 * rows_here)
        pieces = [gat[:, half, mine, :].reshape(ns * 2 * rows_here, half_feats) for half in range(2)]
        step = min(512, half_cols)
        for lo in range(0, cols, step):
            value = sum(
                jnp.dot(
                    piece, wbuf[half * half_feats : (half + 1) * half_feats, lo : lo + step],
                    preferred_element_type=F32,
                )
                for half, piece in enumerate(pieces)
            )
            value = value.astype(BF16).reshape(ns, 2, rows_here, step)
            half, at_col = lo // half_cols, lo % half_cols
            for side in range(2):
                part[at, side, half, :, at_col : at_col + step] = value[:, side].reshape(ns * rows_here, step)
        part_send(at).start()

    def deliver(d, half):
        to = (s + d) % ns
        return remote(
            part.at[p, c, half, span(to, rows_here), :], obuf.at[s, half],
            o_send.at[d, half], o_recv.at[d, half], across(d),
        )

    def add(at):
        part_send(at).wait_recv()
        done = at == p

        def body(count):
            places = (at, nc)[:count]
            sources = [part.at[at, c], psib.at[at]] + [pchn.at[slot] for slot in places]
            for half in range(2):
                for slot in places:
                    arrive(at, b_pair, half, slot)
                step = min(512, half_cols)
                for lo in range(0, half_cols, step):
                    value = functools.reduce(jnp.add, [x[half, :, lo : lo + step].astype(F32) for x in sources])
                    part[at, c, half, :, lo : lo + step] = value.astype(BF16)
                if count < 2:
                    move(at, b_pair, half, True)
                if count > 0:
                    @pl.when(done)
                    def _():
                        for d in range(1, ns):
                            deliver(d, half).start()
                        obuf[s, half] = part[p, c, half, span(s, rows_here), :]

        cases(at, body)

    def projection(i, carry):
        @pl.when(i < nc)
        def _():
            project(i)

        advance(i, add)
        return carry

    lax.fori_loop(0, turns, projection, 0)

    def drain(i, carry):
        for d in range(1, nc):
            query_send(i, d).wait_send()
            query_relay(i, d).wait_send()
        query_twin(i).wait_send()
        for copy in twin_send(i):
            copy.wait_send()
        part_send(i).wait_send()
        for half in range(2):
            move(i, a_pair, half, False)
            move(i, b_pair, half, False)
        return carry

    lax.fori_loop(0, nc, drain, 0)
    for half in range(2):
        for d in range(1, ns):
            spread(d, half).wait_send()
            deliver(d, half).wait_recv()
    for x in range(ns):
        for half in range(2):
            lo = x * cols + half * half_cols
            out_ref[:, lo : lo + half_cols] = obuf[x, half]
    for half in range(2):
        for d in range(1, ns):
            deliver(d, half).wait_send()


def shards(n, ns, queries, probes, keys, values, w_out):
    nc = n // 2
    rows_here, width = queries.shape
    rows = probes.shape[0]
    local_keys = keys.shape[1]
    local_blocks = local_keys // BLOCK
    feats, cols = w_out.shape
    wide = 2 * feats
    heads = feats // DH
    st_rows = max(8, 2 * heads)
    slots = min(nc, 4)
    block_ids = lax.axis_index("mem") * local_blocks + jnp.arange(local_blocks, dtype=jnp.int32)
    probed = jnp.any(probes[:, :, :, None] == block_ids[None, None, None, :], axis=2)
    bias = jnp.where(probed, 0.0, LOW).astype(F32).reshape(rows, nc, 2 * heads * local_blocks)
    bias = jnp.transpose(bias, (1, 0, 2))
    dma = pltpu.SemaphoreType.DMA
    vm = pltpu.VMEM
    flops = 4 * rows * width * local_keys + 2 * ns * rows * feats * cols
    return pl.pallas_call(
        functools.partial(kernel, n, ns),
        out_shape=jax.ShapeDtypeStruct((rows_here, ns * cols), BF16),
        in_specs=[
            pl.BlockSpec(memory_space=pl.ANY),
            pl.BlockSpec(memory_space=pltpu.VMEM),
            pl.BlockSpec(memory_space=pl.ANY),
            pl.BlockSpec(memory_space=pl.ANY),
            pl.BlockSpec(memory_space=pl.ANY),
        ],
        out_specs=pl.BlockSpec(memory_space=pltpu.VMEM),
        scratch_shapes=[
            vm((nc, rows, wide), BF16),
            vm((slots, local_keys, wide), BF16),
            vm((slots, local_keys, wide), BF16),
            vm((feats, cols), BF16),
            vm((nc, 2, 2, rows, feats // 2), BF16),
            vm((nc, 2, st_rows, rows), F32),
            vm((nc, 2, rows, feats // 2), BF16),
            vm((nc, st_rows, rows), F32),
            vm((nc + 1, 2, rows, feats // 2), BF16),
            vm((nc + 1, st_rows, rows), F32),
            vm((ns, 2, rows, feats // 2), BF16),
            vm((nc, 2, 2, ns * rows_here, cols // 2), BF16),
            vm((nc, 2, ns * rows_here, cols // 2), BF16),
            vm((nc + 1, 2, ns * rows_here, cols // 2), BF16),
            vm((ns, 2, rows_here, cols // 2), BF16),
            dma((slots, 2)),
            dma((1,)),
            dma((nc,)),
            dma((nc, nc)),
            dma((nc, nc)),
            dma((nc, nc)),
            dma((nc, nc)),
            dma((nc, 2)),
            dma((nc, 2)),
            dma((nc, 3)),
            dma((nc + 1, 3)),
            dma((ns, 2)),
            dma((ns, 2)),
            dma((nc,)),
            dma((nc,)),
            dma((nc, 2)),
            dma((nc + 1, 2)),
            dma((ns, 2)),
            dma((ns, 2)),
        ],
        compiler_params=pltpu.CompilerParams(
            collective_id=0, has_side_effects=True, vmem_limit_bytes=60 * 1024 * 1024
        ),
        cost_estimate=pl.CostEstimate(
            flops=flops, bytes_accessed=4 * local_keys * width + 2 * feats * cols,
            transcendentals=rows * H * local_keys,
        ),
    )(queries, bias, keys, values, w_out)


def solution(mesh):
    placed = (
        P(("seq", "mem"), None),
        P("seq", None, None),
        P("seq", "mem", None),
        P("seq", "mem", None),
        P("mem", "seq"),
    )
    body = functools.partial(shards, mesh.shape["mem"], mesh.shape["seq"])
    return jax.shard_map(
        body, mesh=mesh, in_specs=placed, out_specs=P(("seq", "mem"), None), check_vma=False
    )
```

```python
import functools

import jax
import jax.numpy as jnp
from jax import lax
from jax.experimental import pallas as pl
from jax.experimental.pallas import tpu as pltpu
from jax.sharding import PartitionSpec as P

H = 64
DH = 128
BLOCK = 256
LOW = -1e30
RATE = DH ** -0.5 * 1.4426950408889634
MESH = pl.DeviceIdType.MESH
F32 = jnp.float32
BF16 = jnp.bfloat16


def kernel(
    n, ns, q_ref, bias_ref, k_ref, v_ref, w_ref, out_ref,
    qg, kbuf, vbuf, wbuf, own, own_st, sib, sib_st, chn, chn_st, fin, gat, part, psib, pchn, obuf,
    kv_sem, w_sem, q_sem, qs_send, qs_recv, rl_send, rl_recv, as_send, as_recv, ac_send, ac_recv,
    g_send, g_recv, bs_send, bs_recv, bc_send, bc_recv, o_send, o_recv,
):
    nc = n // 2
    slots = kbuf.shape[0]
    rows_here, _ = q_ref.shape
    rows = qg.shape[1]
    wide = qg.shape[2]
    feats = wide // 2
    heads = feats // DH
    half_heads = heads // 2
    half_feats = feats // 2
    keys = kbuf.shape[1]
    blocks = keys // BLOCK
    cols = wbuf.shape[1]
    half_cols = cols // 2
    st_rows = own_st.shape[2]
    s = lax.axis_index("seq")
    me = lax.axis_index("mem")
    p = me // 2
    c = me % 2
    twin = (s, p * 2 + 1 - c)

    def peer(d):
        return (s, ((p + d) % nc) * 2 + c)

    def across(d):
        return ((s + d) % ns, me)

    def turn(i):
        return (i % 2) * (nc - 1 - i // 2) + (1 - i % 2) * (i // 2)

    def remote(src, dst, send, recv, to):
        return pltpu.make_async_remote_copy(
            src_ref=src, dst_ref=dst, send_sem=send, recv_sem=recv, device_id=to, device_id_type=MESH
        )

    def span(i, size):
        return pl.ds(pl.multiple_of(i * size, size), size)

    def key_copies(i):
        at = turn(i)
        slot = i % slots
        return (
            pltpu.make_async_copy(k_ref.at[0, :, span(at, wide)], kbuf.at[slot], kv_sem.at[slot, 0]),
            pltpu.make_async_copy(v_ref.at[0, :, span(at, wide)], vbuf.at[slot], kv_sem.at[slot, 1]),
        )

    def own_query(at):
        return pltpu.make_async_copy(
            q_ref.at[:, span(at, wide)], qg.at[at, span(me, rows_here), :], q_sem.at[at]
        )

    def query_send(at, d):
        return remote(
            q_ref.at[:, span(at, wide)], qg.at[at, span(me, rows_here), :],
            qs_send.at[at, d], qs_recv.at[at, d], peer(d),
        )

    def query_twin(at):
        return remote(
            q_ref.at[:, span(at, wide)], qg.at[at, span(me, rows_here), :],
            rl_send.at[at, 0], rl_recv.at[at, 0], twin,
        )

    def query_relay(at, d):
        source = ((p + nc - d) % nc) * 2 + c
        piece = qg.at[at, span(source, rows_here), :]
        return remote(piece, piece, rl_send.at[at, d], rl_recv.at[at, d], twin)

    weight_copy = pltpu.make_async_copy(w_ref, wbuf, w_sem.at[0])

    barrier = pltpu.get_barrier_semaphore()
    for d in range(1, nc):
        pl.semaphore_signal(barrier, inc=1, device_id=peer(d), device_id_type=MESH)
    for d in range(1, ns):
        pl.semaphore_signal(barrier, inc=1, device_id=across(d), device_id_type=MESH)
    pl.semaphore_signal(barrier, inc=1, device_id=twin, device_id_type=MESH)
    pl.semaphore_wait(barrier, nc + ns - 1)

    def start_queries(i, carry):
        at = turn(i)
        for d in range(1, nc):
            query_send(at, d).start()
        query_twin(at).start()
        own_query(at).start()
        return carry

    lax.fori_loop(0, nc, start_queries, 0)
    for i in range(slots):
        for copy in key_copies(i):
            copy.start()
    weight_copy.start()

    def twin_send(at):
        return (
            remote(own.at[at, 1 - c], sib.at[at], as_send.at[at, 0], as_recv.at[at, 0], twin),
            remote(own_st.at[at, 1 - c], sib_st.at[at], as_send.at[at, 1], as_recv.at[at, 1], twin),
        )

    def relay(at):
        for d in range(1, nc):
            query_send(at, d).wait_recv()
            query_relay(at, d).start()

    def attend(i):
        at = turn(i)
        slot = i % slots
        for copy in key_copies(i):
            copy.wait()
        own_query(at).wait()
        query_twin(at).wait_recv()
        for d in range(1, nc):
            query_relay(at, d).wait_recv()

        def raw(x):
            cut = slice(x * DH, (x + 1) * DH)
            return lax.dot_general(
                kbuf[slot, :, cut], qg[at, :, cut], (((1,), (1,)), ((), ())), preferred_element_type=F32
            )

        scores = raw(0)
        for side in range(2):
            for head in range(heads):
                x = side * heads + head
                later = raw(x + 1) if x + 1 < 2 * heads else None
                pieces = [scores[b * BLOCK : (b + 1) * BLOCK] for b in range(blocks)]
                biases = [bias_ref[at, x * blocks + b : x * blocks + b + 1, :] for b in range(blocks)]
                top = functools.reduce(
                    jnp.maximum,
                    [jnp.max(piece, axis=0, keepdims=True) + bias for piece, bias in zip(pieces, biases)],
                )
                shifts = [jnp.where(bias < 0.0, LOW, -top) for bias in biases]
                weights = [jnp.exp2((piece + shift) * RATE) for piece, shift in zip(pieces, shifts)]
                total = functools.reduce(jnp.add, [jnp.sum(w, axis=0, keepdims=True) for w in weights])
                numer = lax.dot_general(
                    vbuf[slot, :, x * DH : (x + 1) * DH],
                    jnp.concatenate([w.astype(BF16) for w in weights], axis=0),
                    (((0,), (0,)), ((), ())), preferred_element_type=F32,
                )
                half, place = head // half_heads, head % half_heads
                own[at, side, half, place * DH : (place + 1) * DH, :] = numer.astype(BF16)
                own_st[at, side, head : head + 1, :] = top
                own_st[at, side, heads + head : heads + head + 1, :] = total
                scores = later
            if 2 * heads < st_rows:
                own_st[at, side, 2 * heads :, :] = jnp.zeros((st_rows - 2 * heads, rows), F32)
            if side == 0:
                @pl.when(i + 1 < nc)
                def _():
                    relay(turn(i + 1))
        for copy in twin_send(at):
            copy.start()

        @pl.when(i + slots < nc)
        def _():
            for copy in key_copies(i + slots):
                copy.start()

    def a_pair(at, half, slot, to):
        made = [
            remote(own.at[at, c, half], chn.at[slot, half], ac_send.at[at, half], ac_recv.at[slot, half], to)
        ]
        if half == 0:
            made.append(remote(own_st.at[at, c], chn_st.at[slot], ac_send.at[at, 2], ac_recv.at[slot, 2], to))
        return made

    def b_pair(at, half, slot, to):
        return [
            remote(part.at[at, c, half], pchn.at[slot, half], bc_send.at[at, half], bc_recv.at[slot, half], to)
        ]

    def move(at, maker, half, begin):
        def go(slot, step):
            for copy in maker(at, half, slot, (s, (p + step) * 2 + c)):
                if begin:
                    copy.start()
                else:
                    copy.wait_send()

        @pl.when(at > p)
        def _():
            go(at, 1)

        @pl.when((at < p) & ((at != p - 1) | (at == 0)))
        def _():
            go(at, -1)

        @pl.when((at < p) & (at == p - 1) & (at > 0))
        def _():
            go(nc, -1)

    def arrive(at, maker, half, slot):
        for copy in maker(at, half, slot, twin):
            copy.wait_recv()

    def cases(at, body):
        ends = ((at > p) & (p == 0)) | ((at < p) & (p == nc - 1))
        both = (at == p) & (p > 0) & (p < nc - 1)

        @pl.when(ends)
        def _():
            body(0)

        @pl.when(jnp.logical_not(ends | both))
        def _():
            body(1)

        @pl.when(both)
        def _():
            body(2)

    def spread(d, half):
        return remote(
            fin.at[half], gat.at[s, half], g_send.at[d, half], g_recv.at[d, half], across(d)
        )

    def merge(at):
        for copy in twin_send(at):
            copy.wait_recv()

        def body(count):
            places = (at, nc)[:count]
            sources = [(own.at[at, c], own_st.at[at, c]), (sib.at[at], sib_st.at[at])]
            for slot in places:
                arrive(at, a_pair, 0, slot)
                sources.append((chn.at[slot], chn_st.at[slot]))
            tops = [st[:heads] for _, st in sources]
            sums = [st[heads : 2 * heads] for _, st in sources]
            top = functools.reduce(jnp.maximum, tops)
            scales = [jnp.exp2((t - top) * RATE) for t in tops]
            total = functools.reduce(jnp.add, [e * t for e, t in zip(scales, sums)])
            done = at == p
            factor = jnp.where(done, 1.0 / total, jnp.ones_like(total))
            scales = [e * factor for e in scales]
            own_st[at, c, :heads] = top
            own_st[at, c, heads : 2 * heads] = total
            for half in range(2):
                if half == 1:
                    for slot in places:
                        arrive(at, a_pair, 1, slot)
                for place in range(half_heads):
                    cut = slice(place * DH, (place + 1) * DH)
                    head = half * half_heads + place
                    value = functools.reduce(
                        jnp.add,
                        [
                            num[half, cut, :].astype(F32) * scale[head : head + 1]
                            for scale, (num, _) in zip(scales, sources)
                        ],
                    )
                    own[at, c, half, cut, :] = value.astype(BF16)
                if count < 2:
                    move(at, a_pair, half, True)
                if count > 0:
                    @pl.when(done)
                    def _():
                        for place in range(half_heads):
                            cut = slice(place * DH, (place + 1) * DH)
                            fin[half, :, cut] = own[p, c, half, cut, :].astype(F32).T.astype(BF16)
                        for d in range(1, ns):
                            spread(d, half).start()
                        gat[s, half] = fin[half]

        cases(at, body)

    turns = nc + nc - nc // 2

    def advance(i, join):
        late = i // nc
        k = (1 - late) * (i // 2) + late * (i - nc + nc // 2)

        def one(side, carry):
            dest = (1 - side) * (nc - 1 - k + p) + side * (k - nc + 1 + p)
            wanted = ((side == 0) & (dest < nc)) | ((side == 1) & (dest >= 0) & (dest < p))

            @pl.when(wanted)
            def _():
                join(dest)

            return carry

        @pl.when((late == 1) | (i % 2 == 1))
        def _():
            lax.fori_loop(0, 2, one, 0)

    def attention(i, carry):
        @pl.when(i < nc)
        def _():
            attend(i)

        advance(i, merge)
        return carry

    relay(turn(0))
    lax.fori_loop(0, turns, attention, 0)

    weight_copy.wait()
    for half in range(2):
        for d in range(1, ns):
            spread(d, half).wait_recv()

    def part_send(at):
        return remote(part.at[at, 1 - c], psib.at[at], bs_send.at[at], bs_recv.at[at], twin)

    def project(i):
        at = turn(i)
        mine = pl.ds(pl.multiple_of(at * 2 * rows_here, 2 * rows_here), 2 * rows_here)
        pieces = [gat[:, half, mine, :].reshape(ns * 2 * rows_here, half_feats) for half in range(2)]
        step = min(512, half_cols)
        for lo in range(0, cols, step):
            value = sum(
                jnp.dot(
                    piece, wbuf[half * half_feats : (half + 1) * half_feats, lo : lo + step],
                    preferred_element_type=F32,
                )
                for half, piece in enumerate(pieces)
            )
            value = value.astype(BF16).reshape(ns, 2, rows_here, step)
            half, at_col = lo // half_cols, lo % half_cols
            for side in range(2):
                part[at, side, half, :, at_col : at_col + step] = value[:, side].reshape(ns * rows_here, step)
        part_send(at).start()

    def deliver(d, half):
        to = (s + d) % ns
        return remote(
            part.at[p, c, half, span(to, rows_here), :], obuf.at[s, half],
            o_send.at[d, half], o_recv.at[d, half], across(d),
        )

    def add(at):
        part_send(at).wait_recv()
        done = at == p

        def body(count):
            places = (at, nc)[:count]
            sources = [part.at[at, c], psib.at[at]] + [pchn.at[slot] for slot in places]
            for half in range(2):
                for slot in places:
                    arrive(at, b_pair, half, slot)
                step = min(512, half_cols)
                for lo in range(0, half_cols, step):
                    value = functools.reduce(jnp.add, [x[half, :, lo : lo + step].astype(F32) for x in sources])
                    part[at, c, half, :, lo : lo + step] = value.astype(BF16)
                if count < 2:
                    move(at, b_pair, half, True)
                if count > 0:
                    @pl.when(done)
                    def _():
                        for d in range(1, ns):
                            deliver(d, half).start()
                        obuf[s, half] = part[p, c, half, span(s, rows_here), :]

        cases(at, body)

    def projection(i, carry):
        @pl.when(i < nc)
        def _():
            project(i)

        advance(i, add)
        return carry

    lax.fori_loop(0, turns, projection, 0)

    def drain(i, carry):
        for d in range(1, nc):
            query_send(i, d).wait_send()
            query_relay(i, d).wait_send()
        query_twin(i).wait_send()
        for copy in twin_send(i):
            copy.wait_send()
        part_send(i).wait_send()
        for half in range(2):
            move(i, a_pair, half, False)
            move(i, b_pair, half, False)
        return carry

    lax.fori_loop(0, nc, drain, 0)
    for half in range(2):
        for d in range(1, ns):
            spread(d, half).wait_send()
            deliver(d, half).wait_recv()
    for x in range(ns):
        for half in range(2):
            lo = x * cols + half * half_cols
            out_ref[:, lo : lo + half_cols] = obuf[x, half]
    for half in range(2):
        for d in range(1, ns):
            deliver(d, half).wait_send()


def shards(n, ns, queries, probes, keys, values, w_out):
    nc = n // 2
    rows_here, width = queries.shape
    rows = probes.shape[0]
    local_keys = keys.shape[1]
    local_blocks = local_keys // BLOCK
    feats, cols = w_out.shape
    wide = 2 * feats
    heads = feats // DH
    st_rows = max(8, 2 * heads)
    slots = min(nc, 4)
    block_ids = lax.axis_index("mem") * local_blocks + jnp.arange(local_blocks, dtype=jnp.int32)
    probed = jnp.any(probes[:, :, :, None] == block_ids[None, None, None, :], axis=2)
    bias = jnp.where(probed, 0.0, LOW).astype(F32)
    bias = jnp.transpose(bias, (1, 2, 0)).reshape(nc, 2 * heads * local_blocks, rows)
    dma = pltpu.SemaphoreType.DMA
    vm = pltpu.VMEM
    flops = 4 * rows * width * local_keys + 2 * ns * rows * feats * cols
    return pl.pallas_call(
        functools.partial(kernel, n, ns),
        out_shape=jax.ShapeDtypeStruct((rows_here, ns * cols), BF16),
        in_specs=[
            pl.BlockSpec(memory_space=pl.ANY),
            pl.BlockSpec(memory_space=pltpu.VMEM),
            pl.BlockSpec(memory_space=pl.ANY),
            pl.BlockSpec(memory_space=pl.ANY),
            pl.BlockSpec(memory_space=pl.ANY),
        ],
        out_specs=pl.BlockSpec(memory_space=pltpu.VMEM),
        scratch_shapes=[
            vm((nc, rows, wide), BF16),
            vm((slots, local_keys, wide), BF16),
            vm((slots, local_keys, wide), BF16),
            vm((feats, cols), BF16),
            vm((nc, 2, 2, feats // 2, rows), BF16),
            vm((nc, 2, st_rows, rows), F32),
            vm((nc, 2, feats // 2, rows), BF16),
            vm((nc, st_rows, rows), F32),
            vm((nc + 1, 2, feats // 2, rows), BF16),
            vm((nc + 1, st_rows, rows), F32),
            vm((2, rows, feats // 2), BF16),
            vm((ns, 2, rows, feats // 2), BF16),
            vm((nc, 2, 2, ns * rows_here, cols // 2), BF16),
            vm((nc, 2, ns * rows_here, cols // 2), BF16),
            vm((nc + 1, 2, ns * rows_here, cols // 2), BF16),
            vm((ns, 2, rows_here, cols // 2), BF16),
            dma((slots, 2)),
            dma((1,)),
            dma((nc,)),
            dma((nc, nc)),
            dma((nc, nc)),
            dma((nc, nc)),
            dma((nc, nc)),
            dma((nc, 2)),
            dma((nc, 2)),
            dma((nc, 3)),
            dma((nc + 1, 3)),
            dma((ns, 2)),
            dma((ns, 2)),
            dma((nc,)),
            dma((nc,)),
            dma((nc, 2)),
            dma((nc + 1, 2)),
            dma((ns, 2)),
            dma((ns, 2)),
        ],
        compiler_params=pltpu.CompilerParams(
            collective_id=0, has_side_effects=True, vmem_limit_bytes=60 * 1024 * 1024
        ),
        cost_estimate=pl.CostEstimate(
            flops=flops, bytes_accessed=4 * local_keys * width + 2 * feats * cols,
            transcendentals=rows * H * local_keys,
        ),
    )(queries, bias, keys, values, w_out)


def solution(mesh):
    placed = (
        P(("seq", "mem"), None),
        P("seq", None, None),
        P("seq", "mem", None),
        P("seq", "mem", None),
        P("mem", "seq"),
    )
    body = functools.partial(shards, mesh.shape["mem"], mesh.shape["seq"])
    return jax.shard_map(
        body, mesh=mesh, in_specs=placed, out_specs=P(("seq", "mem"), None), check_vma=False
    )
```

```python
import functools

import jax
import jax.numpy as jnp
from jax import lax
from jax.experimental import pallas as pl
from jax.experimental.pallas import tpu as pltpu
from jax.sharding import PartitionSpec as P

H = 64
DH = 128
BLOCK = 256
LOW = -1e30
RATE = DH ** -0.5 * 1.4426950408889634
MESH = pl.DeviceIdType.MESH
F32 = jnp.float32
BF16 = jnp.bfloat16


def kernel(
    n, ns, q_ref, bias_ref, k_ref, v_ref, w_ref, out_ref,
    qg, kbuf, vbuf, wbuf, own, own_st, sib, sib_st, chn, chn_st, fin, gat, part, psib, pchn, obuf,
    kv_sem, w_sem, q_sem, qs_send, qs_recv, rl_send, rl_recv, as_send, as_recv, ac_send, ac_recv,
    g_send, g_recv, bs_send, bs_recv, bc_send, bc_recv, o_send, o_recv,
):
    nc = n // 2
    slots = kbuf.shape[0]
    rows_here, _ = q_ref.shape
    rows = qg.shape[1]
    wide = qg.shape[2]
    feats = wide // 2
    heads = feats // DH
    half_heads = heads // 2
    half_feats = feats // 2
    keys = kbuf.shape[1]
    blocks = keys // BLOCK
    cols = wbuf.shape[1]
    fold = ns // 2
    st_rows = own_st.shape[2]
    s = lax.axis_index("seq")
    me = lax.axis_index("mem")
    p = me // 2
    c = me % 2
    twin = (s, p * 2 + 1 - c)

    def peer(d):
        return (s, ((p + d) % nc) * 2 + c)

    def across(d):
        return (((s // 2 + d // 2) % fold) * 2 + (s % 2 + d % 2) % 2, me)

    def origin(d):
        return (((s // 2 + fold - d // 2) % fold) * 2 + (s % 2 + d % 2) % 2, me)

    def turn(i):
        return (i % 2) * (nc - 1 - i // 2) + (1 - i % 2) * (i // 2)

    def remote(src, dst, send, recv, to):
        return pltpu.make_async_remote_copy(
            src_ref=src, dst_ref=dst, send_sem=send, recv_sem=recv, device_id=to, device_id_type=MESH
        )

    def span(i, size):
        return pl.ds(pl.multiple_of(i * size, size), size)

    def key_copies(i):
        at = turn(i)
        slot = i % slots
        return (
            pltpu.make_async_copy(k_ref.at[0, :, span(at, wide)], kbuf.at[slot], kv_sem.at[slot, 0]),
            pltpu.make_async_copy(v_ref.at[0, :, span(at, wide)], vbuf.at[slot], kv_sem.at[slot, 1]),
        )

    def own_query(at):
        return pltpu.make_async_copy(
            q_ref.at[:, span(at, wide)], qg.at[at, span(me, rows_here), :], q_sem.at[at]
        )

    def query_send(at, d):
        return remote(
            q_ref.at[:, span(at, wide)], qg.at[at, span(me, rows_here), :],
            qs_send.at[at, d], qs_recv.at[at, d], peer(d),
        )

    def query_twin(at):
        return remote(
            q_ref.at[:, span(at, wide)], qg.at[at, span(me, rows_here), :],
            rl_send.at[at, 0], rl_recv.at[at, 0], twin,
        )

    def query_relay(at, d):
        source = ((p + nc - d) % nc) * 2 + c
        piece = qg.at[at, span(source, rows_here), :]
        return remote(piece, piece, rl_send.at[at, d], rl_recv.at[at, d], twin)

    weight_copy = pltpu.make_async_copy(w_ref, wbuf, w_sem.at[0])

    barrier = pltpu.get_barrier_semaphore()
    for d in range(1, nc):
        pl.semaphore_signal(barrier, inc=1, device_id=peer(d), device_id_type=MESH)
    for d in range(1, ns):
        pl.semaphore_signal(barrier, inc=1, device_id=across(d), device_id_type=MESH)
    pl.semaphore_signal(barrier, inc=1, device_id=twin, device_id_type=MESH)
    pl.semaphore_wait(barrier, nc + ns - 1)

    def start_queries(i, carry):
        at = turn(i)
        for d in range(1, nc):
            query_send(at, d).start()
        query_twin(at).start()
        own_query(at).start()
        return carry

    lax.fori_loop(0, nc, start_queries, 0)
    for i in range(slots):
        for copy in key_copies(i):
            copy.start()
    weight_copy.start()

    def twin_send(at):
        return (
            remote(own.at[at, 1 - c], sib.at[at], as_send.at[at, 0], as_recv.at[at, 0], twin),
            remote(own_st.at[at, 1 - c], sib_st.at[at], as_send.at[at, 1], as_recv.at[at, 1], twin),
        )

    def relay(at):
        for d in range(1, nc):
            query_send(at, d).wait_recv()
            query_relay(at, d).start()

    def attend(i):
        at = turn(i)
        slot = i % slots
        for copy in key_copies(i):
            copy.wait()
        own_query(at).wait()
        query_twin(at).wait_recv()
        for d in range(1, nc):
            query_relay(at, d).wait_recv()

        def raw(x):
            cut = slice(x * DH, (x + 1) * DH)
            return lax.dot_general(
                kbuf[slot, :, cut], qg[at, :, cut], (((1,), (1,)), ((), ())), preferred_element_type=F32
            )

        scores = raw(0)
        for side in range(2):
            for head in range(heads):
                x = side * heads + head
                later = raw(x + 1) if x + 1 < 2 * heads else None
                pieces = [scores[b * BLOCK : (b + 1) * BLOCK] for b in range(blocks)]
                biases = [bias_ref[at, x * blocks + b : x * blocks + b + 1, :] for b in range(blocks)]
                top = functools.reduce(
                    jnp.maximum,
                    [jnp.max(piece, axis=0, keepdims=True) + bias for piece, bias in zip(pieces, biases)],
                )
                shifts = [jnp.where(bias < 0.0, LOW, -top) for bias in biases]
                weights = [jnp.exp2((piece + shift) * RATE) for piece, shift in zip(pieces, shifts)]
                total = functools.reduce(jnp.add, [jnp.sum(w, axis=0, keepdims=True) for w in weights])
                numer = lax.dot_general(
                    vbuf[slot, :, x * DH : (x + 1) * DH],
                    jnp.concatenate([w.astype(BF16) for w in weights], axis=0),
                    (((0,), (0,)), ((), ())), preferred_element_type=F32,
                )
                half, place = head // half_heads, head % half_heads
                own[at, side, half, place * DH : (place + 1) * DH, :] = numer.astype(BF16)
                own_st[at, side, head : head + 1, :] = top
                own_st[at, side, heads + head : heads + head + 1, :] = total
                scores = later
            if 2 * heads < st_rows:
                own_st[at, side, 2 * heads :, :] = jnp.zeros((st_rows - 2 * heads, rows), F32)
            if side == 0:
                @pl.when(i + 1 < nc)
                def _():
                    relay(turn(i + 1))
        for copy in twin_send(at):
            copy.start()

        @pl.when(i + slots < nc)
        def _():
            for copy in key_copies(i + slots):
                copy.start()

    def a_pair(at, half, slot, to):
        made = [
            remote(own.at[at, c, half], chn.at[slot, half], ac_send.at[at, half], ac_recv.at[slot, half], to)
        ]
        if half == 0:
            made.append(remote(own_st.at[at, c], chn_st.at[slot], ac_send.at[at, 2], ac_recv.at[slot, 2], to))
        return made

    def b_pair(at, half, slot, to):
        return [
            remote(part.at[at, c, half], pchn.at[slot, half], bc_send.at[at, half], bc_recv.at[slot, half], to)
        ]

    def move(at, maker, half, begin):
        def go(slot, step):
            for copy in maker(at, half, slot, (s, (p + step) * 2 + c)):
                if begin:
                    copy.start()
                else:
                    copy.wait_send()

        @pl.when(at > p)
        def _():
            go(at, 1)

        @pl.when((at < p) & ((at != p - 1) | (at == 0)))
        def _():
            go(at, -1)

        @pl.when((at < p) & (at == p - 1) & (at > 0))
        def _():
            go(nc, -1)

    def arrive(at, maker, half, slot):
        for copy in maker(at, half, slot, twin):
            copy.wait_recv()

    def cases(at, body):
        ends = ((at > p) & (p == 0)) | ((at < p) & (p == nc - 1))
        both = (at == p) & (p > 0) & (p < nc - 1)

        @pl.when(ends)
        def _():
            body(0)

        @pl.when(jnp.logical_not(ends | both))
        def _():
            body(1)

        @pl.when(both)
        def _():
            body(2)

    def spread(d, half):
        return remote(
            fin.at[half], gat.at[d, half], g_send.at[d, half], g_recv.at[d, half], across(d)
        )

    def merge(at):
        for copy in twin_send(at):
            copy.wait_recv()

        def body(count):
            places = (at, nc)[:count]
            sources = [(own.at[at, c], own_st.at[at, c]), (sib.at[at], sib_st.at[at])]
            for slot in places:
                arrive(at, a_pair, 0, slot)
                sources.append((chn.at[slot], chn_st.at[slot]))
            tops = [st[:heads] for _, st in sources]
            sums = [st[heads : 2 * heads] for _, st in sources]
            top = functools.reduce(jnp.maximum, tops)
            scales = [jnp.exp2((t - top) * RATE) for t in tops]
            total = functools.reduce(jnp.add, [e * t for e, t in zip(scales, sums)])
            done = at == p
            factor = jnp.where(done, 1.0 / total, jnp.ones_like(total))
            scales = [e * factor for e in scales]
            own_st[at, c, :heads] = top
            own_st[at, c, heads : 2 * heads] = total
            for half in range(2):
                if half == 1:
                    for slot in places:
                        arrive(at, a_pair, 1, slot)
                for place in range(half_heads):
                    cut = slice(place * DH, (place + 1) * DH)
                    head = half * half_heads + place
                    value = functools.reduce(
                        jnp.add,
                        [
                            num[half, cut, :].astype(F32) * scale[head : head + 1]
                            for scale, (num, _) in zip(scales, sources)
                        ],
                    )
                    own[at, c, half, cut, :] = value.astype(BF16)
                if count < 2:
                    move(at, a_pair, half, True)
                if count > 0:
                    @pl.when(done)
                    def _():
                        for place in range(half_heads):
                            cut = slice(place * DH, (place + 1) * DH)
                            fin[half, :, cut] = own[p, c, half, cut, :].astype(F32).T.astype(BF16)
                        for d in range(1, ns):
                            spread(d, half).start()
                        gat[0, half] = fin[half]

        cases(at, body)

    turns = nc + nc - nc // 2

    def stream(k, join):
        def one(side, carry):
            dest = (1 - side) * (nc - 1 - k + p) + side * (k - nc + 1 + p)
            wanted = ((side == 0) & (dest < nc)) | ((side == 1) & (dest >= 0) & (dest < p))

            @pl.when(wanted)
            def _():
                join(dest)

            return carry

        lax.fori_loop(0, 2, one, 0)

    def advance(i, join):
        late = i // nc

        @pl.when((late == 1) | (i % 2 == 1))
        def _():
            stream((1 - late) * (i // 2) + late * (i - nc + nc // 2), join)

    def attention(i, carry):
        @pl.when(i < nc)
        def _():
            attend(i)

        advance(i, merge)
        return carry

    relay(turn(0))
    lax.fori_loop(0, turns, attention, 0)

    def part_send(at, half):
        return remote(
            part.at[at, 1 - c, half], psib.at[at, half], bs_send.at[at, half], bs_recv.at[at, half], twin
        )

    def project(half):
        for d in range(max(1, half * fold), (half + 1) * fold):
            for x in range(2):
                spread(d, x).wait_recv()

        def one(i, carry):
            at = turn(i)
            mine = pl.ds(pl.multiple_of(at * 2 * rows_here, 2 * rows_here), 2 * rows_here)
            pieces = [
                gat[half * fold : (half + 1) * fold, x, mine, :].reshape(fold * 2 * rows_here, half_feats)
                for x in range(2)
            ]
            step = min(512, cols)
            for lo in range(0, cols, step):
                value = sum(
                    jnp.dot(
                        piece, wbuf[x * half_feats : (x + 1) * half_feats, lo : lo + step],
                        preferred_element_type=F32,
                    )
                    for x, piece in enumerate(pieces)
                )
                value = value.astype(BF16).reshape(fold, 2, rows_here, step)
                for side in range(2):
                    part[at, side, half, :, lo : lo + step] = value[:, side].reshape(fold * rows_here, step)
            part_send(at, half).start()
            return carry

        lax.fori_loop(0, nc, one, 0)

    def deliver(d):
        half, place = d // fold, d % fold
        return remote(
            part.at[p, c, half, place * rows_here : (place + 1) * rows_here, :], obuf.at[s],
            o_send.at[d], o_recv.at[d], origin(d),
        )

    def add(half):
        def join(at):
            part_send(at, half).wait_recv()
            done = at == p

            def body(count):
                places = (at, nc)[:count]
                sources = [part.at[at, c], psib.at[at]] + [pchn.at[slot] for slot in places]
                for slot in places:
                    arrive(at, b_pair, half, slot)
                step = min(512, cols)
                for lo in range(0, cols, step):
                    value = functools.reduce(jnp.add, [x[half, :, lo : lo + step].astype(F32) for x in sources])
                    part[at, c, half, :, lo : lo + step] = value.astype(BF16)
                if count < 2:
                    move(at, b_pair, half, True)
                if count > 0:
                    @pl.when(done)
                    def _():
                        for d in range(max(1, half * fold), (half + 1) * fold):
                            deliver(d).start()
                        if half == 0:
                            obuf[s] = part[p, c, 0, :rows_here, :]

            cases(at, body)

        return join

    weight_copy.wait()
    project(0)
    stream(0, add(0))
    project(1)
    stream(0, add(1))

    def summing(k, carry):
        stream(k, add(0))
        stream(k, add(1))
        return carry

    lax.fori_loop(1, nc, summing, 0)

    def drain(i, carry):
        for d in range(1, nc):
            query_send(i, d).wait_send()
            query_relay(i, d).wait_send()
        query_twin(i).wait_send()
        for copy in twin_send(i):
            copy.wait_send()
        for half in range(2):
            part_send(i, half).wait_send()
        for half in range(2):
            move(i, a_pair, half, False)
            move(i, b_pair, half, False)
        return carry

    lax.fori_loop(0, nc, drain, 0)
    for d in range(1, ns):
        for half in range(2):
            spread(d, half).wait_send()
        deliver(d).wait_recv()
    for x in range(ns):
        out_ref[:, x * cols : (x + 1) * cols] = obuf[x]
    for d in range(1, ns):
        deliver(d).wait_send()


def shards(n, ns, queries, probes, keys, values, w_out):
    nc = n // 2
    rows_here, width = queries.shape
    rows = probes.shape[0]
    local_keys = keys.shape[1]
    local_blocks = local_keys // BLOCK
    feats, cols = w_out.shape
    wide = 2 * feats
    heads = feats // DH
    st_rows = max(8, 2 * heads)
    slots = min(nc, 4)
    block_ids = lax.axis_index("mem") * local_blocks + jnp.arange(local_blocks, dtype=jnp.int32)
    probed = jnp.any(probes[:, :, :, None] == block_ids[None, None, None, :], axis=2)
    bias = jnp.where(probed, 0.0, LOW).astype(F32)
    bias = jnp.transpose(bias, (1, 2, 0)).reshape(nc, 2 * heads * local_blocks, rows)
    dma = pltpu.SemaphoreType.DMA
    vm = pltpu.VMEM
    flops = 4 * rows * width * local_keys + 2 * ns * rows * feats * cols
    return pl.pallas_call(
        functools.partial(kernel, n, ns),
        out_shape=jax.ShapeDtypeStruct((rows_here, ns * cols), BF16),
        in_specs=[
            pl.BlockSpec(memory_space=pl.ANY),
            pl.BlockSpec(memory_space=pltpu.VMEM),
            pl.BlockSpec(memory_space=pl.ANY),
            pl.BlockSpec(memory_space=pl.ANY),
            pl.BlockSpec(memory_space=pl.ANY),
        ],
        out_specs=pl.BlockSpec(memory_space=pltpu.VMEM),
        scratch_shapes=[
            vm((nc, rows, wide), BF16),
            vm((slots, local_keys, wide), BF16),
            vm((slots, local_keys, wide), BF16),
            vm((feats, cols), BF16),
            vm((nc, 2, 2, feats // 2, rows), BF16),
            vm((nc, 2, st_rows, rows), F32),
            vm((nc, 2, feats // 2, rows), BF16),
            vm((nc, st_rows, rows), F32),
            vm((nc + 1, 2, feats // 2, rows), BF16),
            vm((nc + 1, st_rows, rows), F32),
            vm((2, rows, feats // 2), BF16),
            vm((ns, 2, rows, feats // 2), BF16),
            vm((nc, 2, 2, ns // 2 * rows_here, cols), BF16),
            vm((nc, 2, ns // 2 * rows_here, cols), BF16),
            vm((nc + 1, 2, ns // 2 * rows_here, cols), BF16),
            vm((ns, rows_here, cols), BF16),
            dma((slots, 2)),
            dma((1,)),
            dma((nc,)),
            dma((nc, nc)),
            dma((nc, nc)),
            dma((nc, nc)),
            dma((nc, nc)),
            dma((nc, 2)),
            dma((nc, 2)),
            dma((nc, 3)),
            dma((nc + 1, 3)),
            dma((ns, 2)),
            dma((ns, 2)),
            dma((nc, 2)),
            dma((nc, 2)),
            dma((nc, 2)),
            dma((nc + 1, 2)),
            dma((ns,)),
            dma((ns,)),
        ],
        compiler_params=pltpu.CompilerParams(
            collective_id=0, has_side_effects=True, vmem_limit_bytes=60 * 1024 * 1024
        ),
        cost_estimate=pl.CostEstimate(
            flops=flops, bytes_accessed=4 * local_keys * width + 2 * feats * cols,
            transcendentals=rows * H * local_keys,
        ),
    )(queries, bias, keys, values, w_out)


def solution(mesh):
    placed = (
        P(("seq", "mem"), None),
        P("seq", None, None),
        P("seq", "mem", None),
        P("seq", "mem", None),
        P("mem", "seq"),
    )
    body = functools.partial(shards, mesh.shape["mem"], mesh.shape["seq"])
    return jax.shard_map(
        body, mesh=mesh, in_specs=placed, out_specs=P(("seq", "mem"), None), check_vma=False
    )
```
